256 devices in a mesh: blk: 64 (over z_hi, y, x), view: 4 (over z_lo, core).
Axes of the slice: x: 4, y: 4, z: 8 (z_hi: 4, z_lo: 2; z = z_hi * 2 + z_lo), core: 2. Of those that a mesh axis runs over, the one named last changes fastest.
Arguments:
- estimate: float32 [1024, 128, 128], P('blk'), may hold values from 0.2 to 5
- recorded: float32 [4, 1024, 128, 128], P('view', 'blk'), may hold values from 0.2 to 5
- offsets: int32 [4, 3], P('view'), may hold values from -16 to 16, as said below
- psf_z: float32 [4, 31], P('view'), may hold values from 0.05 to 1
- psf_y: float32 [4, 31], P('view'), may hold values from 0.05 to 1
- psf_x: float32 [4, 31], P('view'), may hold values from 0.05 to 1
- view_weights: float32 [4], P('view'), may hold values from 0.5 to 2
Outputs:
- deconvolved: float32 [1024, 128, 128], P('blk')
The draws below stay inside these ranges and needn't reach their ends.
Inputs may be any that keep to these rules, and one draw needn't show every extreme that they name: offsets[v, 0] lies within -16 to 16, and in every draw one view has exactly 16 and another exactly -16; offsets[v, 1] and offsets[v, 2] lie within -8 to 8.
All inputs are finite; a program needn't handle non-finite values.
Results may differ from the reference program's by a relative error of at most 0.0001.
Values sent between devices are 32-bit elements; how exact they have to be, the bound alone decides.
No kernel may reach another device: no remote copies, remote signals or barrier semaphores. Data moves between devices by JAX's collectives and lax.ppermute only.
A program may use at most 64 MiB of HBM per device.

```python
import math
import jax
import jax.numpy as jnp
from jax import lax

BZ = 16
BY = 128
BX = 128
TAPS = 31
ITERS = 2
VIEWS = 4
NZ = 1024


def draw_offsets(key, part):
    key = jax.random.fold_in(key, 1)
    key_z, key_pick, key_plane = jax.random.split(key, 3)
    slab = jax.random.randint(key_z, (VIEWS,), -BZ, BZ + 1)
    order = jax.random.permutation(key_pick, VIEWS)
    slab = slab.at[order[0]].set(BZ)
    slab = slab.at[order[1]].set(-BZ)
    plane = jax.random.randint(key_plane, (VIEWS, 2), -8, 9)
    return jnp.concatenate([slab[:, None], plane], axis=1).astype(jnp.int32)


def block_scale(stream_key, extent, cuts, least, high):
    def one(dim, shards_of):
        draws = jax.random.uniform(jax.random.fold_in(jax.random.fold_in(stream_key, 6), dim), (shards_of,), jnp.float32, least / len(cuts), high / len(cuts))
        return jnp.repeat(jnp.exp(draws), extent[dim] // shards_of).reshape((-1,) + (1,) * (len(extent) - dim - 1))

    level = one(*cuts[0])
    for cut in cuts[1:]:
        level = level * one(*cut)
    return level


def setup_inputs(seed: int = 0) -> dict:
    key_list = jax.random.split(jax.random.key(seed), 8)
    return {
        "estimate": jnp.clip(jnp.exp(math.log(5.0) - 3.218876 * jax.random.uniform(key_list[0], (NZ, BY, BX), jnp.float32) ** block_scale(key_list[0], (NZ, BY, BX), ((0, 64),), -0.2, 0.2)), 0.2, 5.0),
        "recorded": jnp.clip(jnp.exp(math.log(5.0) - 3.218876 * jax.random.uniform(key_list[1], (VIEWS, NZ, BY, BX), jnp.float32) ** block_scale(key_list[1], (VIEWS, NZ, BY, BX), ((0, 4), (1, 64)), -0.2, 0.2)), 0.2, 5.0),
        "offsets": draw_offsets(jax.random.fold_in(key_list[7], 71), 0),
        "psf_z": jnp.clip(jnp.exp(math.log(1.0) - 2.9957323 * jax.random.uniform(key_list[3], (VIEWS, TAPS), jnp.float32) ** block_scale(key_list[3], (VIEWS, TAPS), ((0, 4),), -0.2, 0.2)), 0.05, 1.0),
        "psf_y": jnp.clip(jnp.exp(math.log(1.0) - 2.9957323 * jax.random.uniform(key_list[4], (VIEWS, TAPS), jnp.float32) ** block_scale(key_list[4], (VIEWS, TAPS), ((0, 4),), -0.2, 0.2)), 0.05, 1.0),
        "psf_x": jnp.clip(jnp.exp(math.log(1.0) - 2.9957323 * jax.random.uniform(key_list[5], (VIEWS, TAPS), jnp.float32) ** block_scale(key_list[5], (VIEWS, TAPS), ((0, 4),), -0.2, 0.2)), 0.05, 1.0),
        "view_weights": jnp.clip(jnp.exp(math.log(2.0) - 1.3862944 * jax.random.uniform(key_list[6], (VIEWS,), jnp.float32) ** block_scale(key_list[6], (VIEWS,), ((0, 4),), -0.2, 0.2)), 0.5, 2.0),
    }


plane_pad = 8


def band(taps, count):
    width = taps.shape[0]
    half = (width - 1) // 2
    rows = jnp.arange(count, dtype=jnp.int32)[:, None]
    cols = jnp.arange(count, dtype=jnp.int32)[None, :]
    place = cols - rows + half
    inside = (place >= 0) & (place < width)
    return jnp.where(inside, taps[jnp.clip(place, 0, width - 1)], jnp.zeros((), taps.dtype))


def slab_pass(field, taps, adjoint):
    width = taps.shape[0]
    half = (width - 1) // 2
    count = field.shape[0]
    padded = jnp.pad(field, ((half, half), (0, 0), (0, 0)))
    total = jnp.zeros_like(field)
    for tap in range(width):
        start = 2 * half - tap if adjoint else tap
        total = total + taps[tap] * padded[start:start + count]
    return total


def plane_pass(field, mat_y, mat_x):
    inner = jnp.einsum("ij,zjx->zix", mat_y, field, precision=lax.Precision.HIGHEST)
    return jnp.einsum("zyj,ij->zyi", inner, mat_x, precision=lax.Precision.HIGHEST)


def register(field, shift, sign):
    padded = jnp.pad(field, ((BZ, BZ), (plane_pad, plane_pad), (plane_pad, plane_pad)))
    starts = (BZ - sign * shift[0], plane_pad - sign * shift[1], plane_pad - sign * shift[2])
    starts = tuple(jnp.asarray(s).astype(jnp.int32) for s in starts)
    return lax.dynamic_slice(padded, starts, field.shape)


def valid_mask(shape, shift):
    zpos = jnp.arange(shape[0], dtype=jnp.int32)[:, None, None] - shift[0]
    ypos = jnp.arange(shape[1], dtype=jnp.int32)[None, :, None] - shift[1]
    xpos = jnp.arange(shape[2], dtype=jnp.int32)[None, None, :] - shift[2]
    return (zpos >= 0) & (zpos < shape[0]) & (ypos >= 0) & (ypos < shape[1]) & (xpos >= 0) & (xpos < shape[2])


def reference(estimate, recorded, offsets, psf_z, psf_y, psf_x, view_weights):
    views = recorded.shape[0]
    wsum = jnp.sum(view_weights)
    for step in range(ITERS):
        total = jnp.zeros_like(estimate)
        for view in range(views):
            taps_z = psf_z[view] / jnp.sum(psf_z[view])
            taps_y = psf_y[view] / jnp.sum(psf_y[view])
            taps_x = psf_x[view] / jnp.sum(psf_x[view])
            mat_y = band(taps_y, estimate.shape[1])
            mat_x = band(taps_x, estimate.shape[2])
            blurred = plane_pass(slab_pass(estimate, taps_z, False), mat_y, mat_x)
            forward = register(blurred, offsets[view], 1)
            valid = valid_mask(estimate.shape, offsets[view])
            safe = jnp.where(valid, forward, jnp.ones((), jnp.float32))
            ratio = jnp.where(valid, recorded[view] / safe, jnp.zeros((), jnp.float32))
            back = register(ratio, offsets[view], -1)
            back = plane_pass(slab_pass(back, taps_z, True), mat_y.T, mat_x.T)
            total = total + view_weights[view] * back
        estimate = estimate * total / wsum
    return estimate
```

```python
import jax
import jax.numpy as jnp
from jax import lax
from jax.experimental import pallas as pl
from jax.experimental.pallas import tpu as pltpu
from jax.sharding import PartitionSpec as P

ITERS = 2
TAPS = 31
HALF = 15
VIEWS = 4
BZ = 16
ROWS = 32
EXT = 64
LANES = 128
EDGE = 16
LAYERS = BZ + 2 * HALF
AXES = ("blk", "view")
HZ, HY, HX, WZ, MISC = 0, 1, 2, 3, 4
F32 = jnp.float32
BF16 = jnp.bfloat16

CELLS = [(z, y, x, v) for z in range(4) for y in range(4) for x in range(4) for v in range(4)]


def device(z, y, x, v):
    return ((z * 4 + y) * 4 + x) * 4 + v


PATH = ((0, 0), (1, 0), (1, 1), (2, 1), (2, 0), (3, 0), (3, 1), (0, 1))


def place(block, r):
    z, chip, core = block // 16, (block // 2) % 8, block % 2
    y, z_lo = PATH[chip]
    return device(z, y, r, 2 * z_lo + (core ^ (chip % 2)))


def spread(x, j):
    perm = [(device(z, y, c, v), place(16 * z + 4 * y + c, (v + j) % 4)) for z, y, c, v in CELLS]
    return lax.ppermute(x, AXES, perm)


def collect(x, j):
    perm = [(place(16 * z + 4 * y + q, r), device(z, y, q, (r + j) % 4)) for z, y, r, q in CELLS]
    return lax.ppermute(x, AXES, perm)


def view_swap(x, mask):
    return lax.ppermute(x, AXES, [(device(z, y, c, v), device(z, y, c, v ^ mask)) for z, y, c, v in CELLS])


def to_layer(x, step):
    perm = [(place(b, r), place((b + step) % 64, r)) for b in range(64) for r in range(4)]
    return lax.ppermute(x, AXES, perm)


def to_row(x, step):
    perm = [(place(b, r), place(b, (r + step) % 4)) for b in range(64) for r in range(4)]
    return lax.ppermute(x, AXES, perm)


def position():
    blk, view = lax.axis_index("blk"), lax.axis_index("view")
    y = lax.rem(lax.div(blk, 4), 4)
    near = jnp.where(y < 2, y, y + 2)
    far = jnp.where(y == 0, 7, jnp.where(y == 3, 6, y + 1))
    chip = jnp.where(view < 2, near, far)
    core = (view & 1) ^ (chip & 1)
    return view, lax.rem(blk, 4), lax.div(blk, 16) * 16 + 2 * chip + core


def vmem():
    return pl.BlockSpec(memory_space=pltpu.VMEM)


def smem():
    return pl.BlockSpec(memory_space=pltpu.SMEM)


def hbm():
    return pl.BlockSpec(memory_space=pl.ANY)


def call(body, outs, args, specs, scratch, flops, out_specs=None):
    size = sum(a.size * a.dtype.itemsize for a in args)
    return pl.pallas_call(
        body,
        out_shape=outs,
        in_specs=specs,
        out_specs=out_specs or jax.tree.map(lambda _: vmem(), outs),
        scratch_shapes=scratch,
        compiler_params=pltpu.CompilerParams(vmem_limit_bytes=48 * 1024 * 1024),
        cost_estimate=pl.CostEstimate(flops=flops, bytes_accessed=size, transcendentals=0),
    )(*args)


def shape(*dims, dtype=F32):
    return jax.ShapeDtypeStruct(dims, dtype)


def iota(dims, axis):
    return lax.broadcasted_iota(jnp.int32, dims, axis)


def pieces(x):
    high = x.astype(BF16)
    low = (x - high.astype(F32)).astype(BF16)
    return high, low


def prologue_body(offsets, weight, est, rec, psf_z, psf_y, psf_x, ext, o0, o1, o2, o3, held, moved, sems, sem):
    view = lax.axis_index("view")
    step = BZ // 4
    parts = [
        pltpu.make_async_copy(rec.at[0, pl.ds(k * step, step)], held.at[pl.ds(k * step, step)], sems.at[k])
        for k in range(4)
    ]
    for part in parts:
        part.start()

    def window(k):
        first = max(0, k * ROWS - EDGE)
        size = min(LANES, (k + 1) * ROWS + EDGE) - first
        skip = first - (k * ROWS - EDGE)
        return pltpu.make_async_copy(est.at[:, pl.ds(first, size)], ext.at[:, pl.ds(skip, size)], sem)

    for k in range(VIEWS):

        @pl.when(view == k)
        def _(k=k):
            window(k).start()
            if k == 0:
                ext[:, :EDGE, :] = jnp.zeros((BZ, EDGE, LANES), F32)
            if k == VIEWS - 1:
                ext[:, EXT - EDGE :, :] = jnp.zeros((BZ, EDGE, LANES), F32)

    dy, dx = offsets[0, 1], offsets[0, 2]
    row = iota((LANES, LANES), 0) + dy
    col = iota((LANES, LANES), 1) + dx
    inside = (row >= 0) & (row < LANES) & (col >= 0) & (col < LANES)
    back_y = lax.rem(LANES - dy, LANES)
    back_x = lax.rem(LANES - dx, LANES)

    for k, part in enumerate(parts):
        part.wait()

        @pl.loop(k * step, (k + 1) * step)
        def _(z):
            plane = pltpu.roll(pltpu.roll(held[z], back_y, 0), back_x, 1)
            moved[z] = jnp.where(inside, plane, 0.0)

    hz, hy, hx = (t[...] / jnp.sum(t[...], axis=1, keepdims=True) for t in (psf_z, psf_y, psf_x))
    lane = iota((1, LANES), 1)
    misc = jnp.where(lane == 0, weight[0], jnp.where(lane == 1, offsets[0, 0].astype(F32), 0.0))
    for j, out in enumerate((o0, o1, o2, o3)):
        start = pl.multiple_of(lax.rem(view + j, VIEWS) * ROWS, ROWS)
        out[:BZ] = moved[:, pl.ds(start, ROWS), :]
        out[BZ] = jnp.zeros((ROWS, LANES), F32)
        out[BZ, HZ : HZ + 1, :TAPS] = hz
        out[BZ, HY : HY + 1, :TAPS] = hy
        out[BZ, HX : HX + 1, :TAPS] = hx
        out[BZ, WZ : WZ + 1, :TAPS] = weight[0] * hz
        out[BZ, MISC : MISC + 1, :] = misc

    for k in range(VIEWS):

        @pl.when(view == k)
        def _(k=k):
            window(k).wait()


def shift_of(taps, v):
    return taps[v, MISC, 1].astype(jnp.int32)


def pack_body(a0, a1, a2, a3, up, down, rec, taps, held, sems, tap_sems):
    blocks = (a0, a1, a2, a3)
    data = [pltpu.make_async_copy(a.at[pl.ds(0, BZ)], held.at[v], sems.at[v]) for v, a in enumerate(blocks)]
    rows = [
        pltpu.make_async_copy(a.at[BZ, pl.ds(0, 8)], taps.at[v], tap_sems.at[v]) for v, a in enumerate(blocks)
    ]
    for copy in rows + data:
        copy.start()
    for out in (up, down):
        out[BZ:] = jnp.zeros((2 * BZ, ROWS, LANES), F32)
    n_up, n_down = jnp.int32(0), jnp.int32(0)
    for v in range(VIEWS):
        rows[v].wait()
        data[v].wait()
        dz = shift_of(taps, v)

        @pl.when(dz < 0)
        def _(v=v, n=n_up):
            up[pl.ds(n * BZ, BZ)] = held[v]

        @pl.when(dz > 0)
        def _(v=v, n=n_down):
            down[pl.ds(n * BZ, BZ)] = held[v]

        n_up = n_up + jnp.where(dz < 0, 1, 0)
        n_down = n_down + jnp.where(dz > 0, 1, 0)

        @pl.loop(0, BZ)
        def _(i, v=v, dz=dz):
            src = i + dz
            rec[v, i] = jnp.where((src >= 0) & (src < BZ), held[v, jnp.clip(src, 0, BZ - 1)], 0.0)


def bands_body(taps, wy_f, wy_b, wx_f, wx_b):
    dims = (ROWS, 4 * EXT)
    lane = iota(dims, 1)
    gap = (lane & (EXT - 1)) - iota(dims, 0) - 1
    for v in range(VIEWS):
        band = jnp.zeros(dims, F32)
        for a in range(TAPS):
            band = jnp.where(gap == a, taps[v, HY, a], band)
        high = band.astype(BF16).astype(F32)
        wy_f[v * ROWS : (v + 1) * ROWS, :] = jnp.where(lane < 2 * EXT, high, band - high).astype(BF16)

    dims = (EXT, LANES)
    lane = iota(dims, 1)
    gap = iota(dims, 0) - (lane & (ROWS - 1)) - 1
    band = jnp.zeros(dims, F32)
    for a in range(TAPS):
        tap = jnp.zeros((1, LANES), F32)
        for v in range(VIEWS):
            tap = jnp.where(iota((1, LANES), 1) >= v * ROWS, taps[v, HY, a], tap)
        band = jnp.where(gap == a, tap, band)
    high, low = pieces(band)
    wy_b[...] = jnp.concatenate([jnp.concatenate([high, high], 1), jnp.concatenate([low, low], 1)], 0)

    dims = (LANES, LANES)
    gap = iota(dims, 0) - iota(dims, 1)
    for v in range(VIEWS):
        for out, sign in ((wx_f, 1), (wx_b, -1)):
            band = jnp.zeros(dims, F32)
            for a in range(TAPS):
                band = jnp.where(gap == sign * (a - HALF), taps[v, HX, a], band)
            high, low = pieces(band)
            part = jnp.concatenate([high, low], 1)
            out[v] = jnp.concatenate([part, part], 0)


def forward_body(taps, before, own, after, wy_f, wx_f, out, inner, summed):
    _, _, block = position()

    def layer(k):
        if k < HALF:
            return jnp.where(block > 0, before[k + 1], 0.0)
        if k < HALF + BZ:
            return own[k - HALF]
        return jnp.where(block < 63, after[k - HALF - BZ], 0.0)

    for p in range(LAYERS // 2):
        high, low = pieces(jnp.concatenate([layer(2 * p), layer(2 * p + 1)], 1))
        data = jnp.concatenate([high, low, high, low], 0)
        done = jnp.dot(wy_f[...], data, preferred_element_type=F32)
        for v in range(VIEWS):
            rows = done[v * ROWS : (v + 1) * ROWS]
            inner[v, 2 * p] = rows[:, :LANES]
            inner[v, 2 * p + 1] = rows[:, LANES:]

    @pl.loop(0, VIEWS * 4)
    def _(n):
        v = lax.div(n, 4)
        rows = pl.ds(pl.multiple_of(lax.rem(n, 4) * 8, 8), 8)
        hz = [taps[v, HZ, a] for a in range(TAPS)]
        acc = [None] * BZ
        for k in range(LAYERS):
            x = inner[v, k, rows, :]
            for i in range(max(0, k - TAPS + 1), min(BZ - 1, k) + 1):
                term = hz[k - i] * x
                acc[i] = term if acc[i] is None else acc[i] + term
        for i in range(BZ):
            summed[v, i, rows, :] = acc[i]

    for v in range(VIEWS):
        high, low = pieces(summed[v].reshape(BZ * ROWS, LANES))
        done = jnp.dot(jnp.concatenate([high, low], 1), wx_f[v], preferred_element_type=F32)
        out[v] = (done[:, :LANES] + done[:, LANES:]).reshape(BZ, ROWS, LANES)


def back_body(taps, fwd, rec, wx_b, wy_b, before, own, after, inner, spread_z):
    for v in range(VIEWS):
        ratio = (rec[v] / fwd[v]).reshape(BZ * ROWS, LANES)
        high, low = pieces(ratio)
        done = jnp.dot(jnp.concatenate([high, low], 1), wx_b[v], preferred_element_type=F32)
        inner[v] = (done[:, :LANES] + done[:, LANES:]).reshape(BZ, ROWS, LANES)

    @pl.loop(0, VIEWS * 4)
    def _(n):
        v = lax.div(n, 4)
        rows = pl.ds(pl.multiple_of(lax.rem(n, 4) * 8, 8), 8)
        place_rows = pl.ds(pl.multiple_of(n * 8, 8), 8)
        hz = [taps[v, WZ, a] for a in range(TAPS)]
        x = [inner[v, i, rows, :] for i in range(BZ)]
        for k in range(LAYERS):
            acc = None
            for i in range(max(0, k - TAPS + 1), min(BZ - 1, k) + 1):
                term = hz[k - i] * x[i]
                acc = term if acc is None else acc + term
            spread_z[k, place_rows, :] = acc

    def store(k, value):
        if k < HALF:
            before[k] = value
        elif k < HALF + BZ:
            own[k - HALF] = value
        else:
            after[k - HALF - BZ] = value

    for p in range(LAYERS // 2):
        high, low = pieces(jnp.concatenate([spread_z[2 * p], spread_z[2 * p + 1]], 1))
        done = jnp.dot(wy_b[...], jnp.concatenate([high, low], 0), preferred_element_type=F32)
        both = done[:EXT] + done[EXT:]
        store(2 * p, both[:, :LANES])
        store(2 * p + 1, both[:, LANES:])


def first_back_body(taps, fwd, part, lower, upper, wx_b, wy_b, *rest):
    before, own, after, rec, low, high, sems, inner, spread_z = rest
    _, _, block = position()
    copies = [pltpu.make_async_copy(lower, low, sems.at[0]), pltpu.make_async_copy(upper, high, sems.at[1])]
    for copy in copies:
        copy.start()
    for copy in copies:
        copy.wait()
    n_up, n_down = jnp.int32(0), jnp.int32(0)
    for v in range(VIEWS):
        dz = shift_of(taps, v)

        @pl.loop(0, BZ)
        def _(i, v=v, dz=dz, n_up=n_up, n_down=n_down):
            src = i + dz
            place_z = block * BZ + src
            x = part[v, i]
            x = jnp.where(src < 0, low[jnp.clip(n_up * BZ + src + BZ, 0, 3 * BZ - 1)], x)
            x = jnp.where(src >= BZ, high[jnp.clip(n_down * BZ + src - BZ, 0, 3 * BZ - 1)], x)
            rec[v, i] = jnp.where((place_z >= 0) & (place_z < 64 * BZ), x, 0.0)

        n_up = n_up + jnp.where(dz < 0, 1, 0)
        n_down = n_down + jnp.where(dz > 0, 1, 0)

    back_body(taps, fwd, rec, wx_b, wy_b, before, own, after, inner, spread_z)


def add_layers(own, from_prev, from_next, cut):
    _, _, block = position()
    out = []
    for i in range(BZ):
        value = own[i, cut]
        if i < HALF:
            value = value + jnp.where(block > 0, from_prev[i, cut], 0.0)
        if i > 0:
            value = value + jnp.where(block < 63, from_next[i - 1, cut], 0.0)
        out.append(value)
    return out


def halves_body(own, from_prev, from_next, low, high):
    for out, cut in ((low, slice(0, ROWS)), (high, slice(ROWS, EXT))):
        for i, value in enumerate(add_layers(own, from_prev, from_next, cut)):
            out[i] = value


def edges_body(own, from_prev, from_next, low, middle, high):
    cuts = (slice(0, EDGE), slice(EDGE, EXT - EDGE), slice(EXT - EDGE, EXT))
    for out, cut in zip((low, middle, high), cuts):
        for i, value in enumerate(add_layers(own, from_prev, from_next, cut)):
            out[i] = value


def view_sum(taps):
    return taps[0, MISC, 0] + taps[1, MISC, 0] + taps[2, MISC, 0] + taps[3, MISC, 0]


def window_body(taps, ext, low, high, from_prev, from_next, out):
    _, r, _ = position()
    wsum = view_sum(taps)
    for i in range(BZ):
        total = low[i] + jnp.where(r > 0, from_prev[i], 0.0)
        out[i, :ROWS] = ext[i, :ROWS] * total / wsum
        total = high[i] + jnp.where(r < 3, from_next[i], 0.0)
        out[i, ROWS:] = ext[i, ROWS:] * total / wsum


def last_body(taps, ext, middle, from_prev, from_next, out):
    _, r, _ = position()
    wsum = view_sum(taps)
    for i in range(BZ):
        total = middle[i, :EDGE] + jnp.where(r > 0, from_prev[i], 0.0)
        out[i, :EDGE] = ext[i, EDGE:ROWS] * total / wsum
        total = middle[i, EDGE:] + jnp.where(r < 3, from_next[i], 0.0)
        out[i, EDGE:] = ext[i, ROWS : EXT - EDGE] * total / wsum


def join_body(c0, c1, c2, c3, out):
    view = lax.axis_index("view")
    for mask, chunk in enumerate((c0, c1, c2, c3)):
        start = pl.multiple_of((view ^ mask) * ROWS, ROWS)
        out[:, pl.ds(start, ROWS), :] = chunk[...]


BLOCK = (VIEWS, BZ, ROWS, LANES)
INNER = (VIEWS, LAYERS, ROWS, LANES)
SPREAD = (LAYERS, LANES, LANES)
WINDOW = (BZ, EXT, LANES)
HALO = (HALF, EXT, LANES)
QUARTER = (BZ, ROWS, LANES)
PACKED = (3 * BZ, ROWS, LANES)
STRIP = (BZ, EDGE, LANES)


def per_device(estimate, recorded, offsets, psf_z, psf_y, psf_x, view_weights):
    with jax.named_scope("prologue"):
        ext, *chunks = call(
            prologue_body,
            (shape(*WINDOW),) + (shape(BZ + 1, ROWS, LANES),) * 4,
            (offsets, view_weights, estimate, recorded, psf_z, psf_y, psf_x),
            [smem(), smem(), hbm(), hbm()] + [vmem()] * 3,
            [
                pltpu.VMEM((BZ, LANES, LANES), F32),
                pltpu.VMEM((BZ, LANES, LANES), F32),
                pltpu.SemaphoreType.DMA((4,)),
                pltpu.SemaphoreType.DMA,
            ],
            10_000_000,
        )
    with jax.named_scope("spread"):
        ext = spread(ext, 0)
        mine = [spread(c, j) for j, c in enumerate(chunks)]
    with jax.named_scope("shift"):
        up, down, part, taps = call(
            pack_body,
            (shape(*PACKED), shape(*PACKED), shape(*BLOCK), shape(VIEWS, 8, LANES)),
            tuple(mine),
            [hbm()] * 4,
            [pltpu.VMEM(BLOCK, F32), pltpu.SemaphoreType.DMA((4,)), pltpu.SemaphoreType.DMA((4,))],
            10_000_000,
            (vmem(), vmem(), vmem(), smem()),
        )
        lower = to_layer(up, 1)
        upper = to_layer(down, -1)

    with jax.named_scope("bands"):
        wy_f, wy_b, wx_f, wx_b = call(
            bands_body,
            (
                shape(LANES, 4 * EXT, dtype=BF16),
                shape(LANES, 2 * LANES, dtype=BF16),
                shape(VIEWS, 2 * LANES, 2 * LANES, dtype=BF16),
                shape(VIEWS, 2 * LANES, 2 * LANES, dtype=BF16),
            ),
            (taps,),
            [smem()],
            [],
            30_000_000,
        )

    rec = None
    for step in range(ITERS):
        with jax.named_scope("layers_in"):
            before = to_layer(ext, 1)
            after = to_layer(ext, -1)
        with jax.named_scope("forward"):
            fwd = call(
                forward_body,
                shape(*BLOCK),
                (taps, before, ext, after, wy_f, wx_f),
                [smem()] + [vmem()] * 5,
                [pltpu.VMEM(INNER, F32), pltpu.VMEM(BLOCK, F32)],
                2_000_000_000,
            )
        with jax.named_scope("back"):
            outs = (shape(*HALO), shape(*WINDOW), shape(*HALO))
            scratch = [pltpu.VMEM(BLOCK, F32), pltpu.VMEM(SPREAD, F32)]
            if rec is None:
                c_before, c_own, c_after, rec = call(
                    first_back_body,
                    outs + (shape(*BLOCK),),
                    (taps, fwd, part, lower, upper, wx_b, wy_b),
                    [smem(), vmem(), vmem(), hbm(), hbm(), vmem(), vmem()],
                    [pltpu.VMEM(PACKED, F32), pltpu.VMEM(PACKED, F32), pltpu.SemaphoreType.DMA((2,))] + scratch,
                    2_000_000_000,
                )
            else:
                c_before, c_own, c_after = call(
                    back_body,
                    outs,
                    (taps, fwd, rec, wx_b, wy_b),
                    [smem()] + [vmem()] * 4,
                    scratch,
                    2_000_000_000,
                )
        with jax.named_scope("layers_out"):
            from_next = to_layer(c_before, -1)
            from_prev = to_layer(c_after, 1)
        if step < ITERS - 1:
            with jax.named_scope("rows"):
                low, high = call(
                    halves_body, (shape(*QUARTER),) * 2, (c_own, from_prev, from_next), [vmem()] * 3, [], 1_000_000
                )
                row_prev = to_row(high, 1)
                row_next = to_row(low, -1)
                ext = call(
                    window_body,
                    shape(*WINDOW),
                    (taps, ext, low, high, row_prev, row_next),
                    [smem()] + [vmem()] * 5,
                    [],
                    1_000_000,
                )
        else:
            with jax.named_scope("rows"):
                low, middle, high = call(
                    edges_body,
                    (shape(*STRIP), shape(*QUARTER), shape(*STRIP)),
                    (c_own, from_prev, from_next),
                    [vmem()] * 3,
                    [],
                    1_000_000,
                )
                row_prev = to_row(high, 1)
                row_next = to_row(low, -1)
                own = call(
                    last_body,
                    shape(*QUARTER),
                    (taps, ext, middle, row_prev, row_next),
                    [smem()] + [vmem()] * 4,
                    [],
                    1_000_000,
                )

    with jax.named_scope("result"):
        c0 = collect(own, 0)
        c1 = view_swap(c0, 1)
        c2 = view_swap(c0, 2)
        c3 = view_swap(c2, 1)
        return call(join_body, shape(BZ, LANES, LANES), (c0, c1, c2, c3), [vmem()] * 4, [], 1_000_000)


def solution(mesh):
    in_specs = (
        P("blk", None, None),
        P("view", "blk", None, None),
        P("view", None),
        P("view", None),
        P("view", None),
        P("view", None),
        P("view"),
    )
    out_specs = P("blk", None, None)
    return jax.shard_map(
        per_device, mesh=mesh, in_specs=in_specs, out_specs=out_specs, check_vma=False
    )
```

```python
import jax
import jax.numpy as jnp
from jax import lax
from jax.experimental import pallas as pl
from jax.experimental.pallas import tpu as pltpu
from jax.sharding import PartitionSpec as P

ITERS = 2
TAPS = 31
HALF = 15
VIEWS = 4
BZ = 16
ROWS = 32
FLAT = BZ * ROWS
EXT = 64
LANES = 128
EDGE = 16
LAYERS = BZ + 2 * HALF
AXES = ("blk", "view")
HZ, HY, HX, WZ, MISC = 0, 1, 2, 3, 4
F32 = jnp.float32
BF16 = jnp.bfloat16

CELLS = [(z, y, x, v) for z in range(4) for y in range(4) for x in range(4) for v in range(4)]


def device(z, y, x, v):
    return ((z * 4 + y) * 4 + x) * 4 + v


PATH = ((0, 0), (1, 0), (1, 1), (2, 1), (2, 0), (3, 0), (3, 1), (0, 1))


def place(block, r):
    z, chip, core = block // 16, (block // 2) % 8, block % 2
    y, z_lo = PATH[chip]
    return device(z, y, r, 2 * z_lo + (core ^ (chip % 2)))


FAR = (1, 3, 0, 2)


def quarter_of(q, v, j):
    return (q + FAR[v ^ j]) % 4


def spread(x, j):
    perm = [(device(z, y, q, v), place(16 * z + 4 * y + q, quarter_of(q, v, j))) for z, y, q, v in CELLS]
    return lax.ppermute(x, AXES, perm)


def collect(x, j):
    perm = [(place(16 * z + 4 * y + q, quarter_of(q, v, j)), device(z, y, q, v)) for z, y, q, v in CELLS]
    return lax.ppermute(x, AXES, perm)


def view_swap(x, mask):
    return lax.ppermute(x, AXES, [(device(z, y, c, v), device(z, y, c, v ^ mask)) for z, y, c, v in CELLS])


def to_layer(x, step):
    perm = [(place(b, r), place((b + step) % 64, r)) for b in range(64) for r in range(4)]
    return lax.ppermute(x, AXES, perm)


def to_row(x, step):
    perm = [(place(b, r), place(b, (r + step) % 4)) for b in range(64) for r in range(4)]
    return lax.ppermute(x, AXES, perm)


def position():
    blk, view = lax.axis_index("blk"), lax.axis_index("view")
    y = lax.rem(lax.div(blk, 4), 4)
    near = jnp.where(y < 2, y, y + 2)
    far = jnp.where(y == 0, 7, jnp.where(y == 3, 6, y + 1))
    chip = jnp.where(view < 2, near, far)
    core = (view & 1) ^ (chip & 1)
    return view, lax.rem(blk, 4), lax.div(blk, 16) * 16 + 2 * chip + core


def quarter_at(j):
    q = lax.rem(lax.axis_index("blk"), 4)
    slot = lax.axis_index("view") ^ j
    far = jnp.where(slot == 0, 1, jnp.where(slot == 1, 3, jnp.where(slot == 2, 0, 2)))
    return lax.rem(q + far, 4)


def view_at(j):
    _, r, block = position()
    far = lax.rem(r - lax.rem(block, 4) + 4, 4)
    return jnp.where(far == 1, 0, jnp.where(far == 3, 1, jnp.where(far == 0, 2, 3))) ^ j


def vmem():
    return pl.BlockSpec(memory_space=pltpu.VMEM)


def smem():
    return pl.BlockSpec(memory_space=pltpu.SMEM)


def hbm():
    return pl.BlockSpec(memory_space=pl.ANY)


def call(body, outs, args, specs, scratch, flops, out_specs=None, mib=48):
    size = sum(a.size * a.dtype.itemsize for a in args)
    return pl.pallas_call(
        body,
        out_shape=outs,
        in_specs=specs,
        out_specs=out_specs or jax.tree.map(lambda _: vmem(), outs),
        scratch_shapes=scratch,
        compiler_params=pltpu.CompilerParams(vmem_limit_bytes=mib * 1024 * 1024),
        cost_estimate=pl.CostEstimate(flops=flops, bytes_accessed=size, transcendentals=0),
    )(*args)


def shape(*dims, dtype=F32):
    return jax.ShapeDtypeStruct(dims, dtype)


def iota(dims, axis):
    return lax.broadcasted_iota(jnp.int32, dims, axis)


def pieces(x):
    high = x.astype(BF16)
    low = (x - high.astype(F32)).astype(BF16)
    return high, low


def start_body(est, ext, sem):
    def window(k):
        first = max(0, k * ROWS - EDGE)
        size = min(LANES, (k + 1) * ROWS + EDGE) - first
        skip = first - (k * ROWS - EDGE)
        return pltpu.make_async_copy(est.at[:, pl.ds(first, size)], ext.at[:, pl.ds(skip, size)], sem)

    for k in range(VIEWS):

        @pl.when(quarter_at(0) == k)
        def _(k=k):
            window(k).start()
            if k == 0:
                ext[:, :EDGE, :] = jnp.zeros((BZ, EDGE, LANES), F32)
            if k == VIEWS - 1:
                ext[:, EXT - EDGE :, :] = jnp.zeros((BZ, EDGE, LANES), F32)
            window(k).wait()


def planes_body(offsets, weight, rec, psf_z, psf_y, psf_x, o0, o1, o2, o3, moved):
    dy, dx = offsets[0, 1], offsets[0, 2]
    row = iota((LANES, LANES), 0) + dy
    col = iota((LANES, LANES), 1) + dx
    inside = (row >= 0) & (row < LANES) & (col >= 0) & (col < LANES)
    back_y = lax.rem(LANES - dy, LANES)
    back_x = lax.rem(LANES - dx, LANES)

    @pl.loop(0, BZ)
    def _(z):
        plane = pltpu.roll(pltpu.roll(rec[0, z], back_y, 0), back_x, 1)
        moved[z] = jnp.where(inside, plane, 0.0)

    hz, hy, hx = (t[...] / jnp.sum(t[...], axis=1, keepdims=True) for t in (psf_z, psf_y, psf_x))
    lane = iota((1, LANES), 1)
    misc = jnp.where(lane == 0, weight[0], jnp.where(lane == 1, offsets[0, 0].astype(F32), 0.0))
    for j, out in enumerate((o0, o1, o2, o3)):
        start = pl.multiple_of(quarter_at(j) * ROWS, ROWS)
        out[:FLAT] = moved[:, pl.ds(start, ROWS), :].reshape(FLAT, LANES)
        out[FLAT:] = jnp.zeros((8, LANES), F32)
        for row, value in ((HZ, hz), (HY, hy), (HX, hx), (WZ, weight[0] * hz)):
            out[FLAT + row : FLAT + row + 1, :TAPS] = value
        out[FLAT + MISC : FLAT + MISC + 1, :] = misc


def shift_of(taps, v):
    return taps[v, MISC, 1].astype(jnp.int32)


def pack_body(a0, a1, a2, a3, up, down, taps, held, sems, tap_sems):
    blocks = (a0, a1, a2, a3)
    data, rows = [], []
    for j, a in enumerate(blocks):
        data.append(pltpu.make_async_copy(a.at[pl.ds(0, FLAT)], held.at[view_at(j)], sems.at[j]))
        rows.append(pltpu.make_async_copy(a.at[pl.ds(FLAT, 8)], taps.at[view_at(j)], tap_sems.at[j]))
    for copy in rows + data:
        copy.start()
    for copy in rows + data:
        copy.wait()
    for out in (up, down):
        out[FLAT:] = jnp.zeros((2 * FLAT, LANES), F32)
    n_up, n_down = jnp.int32(0), jnp.int32(0)
    for v in range(VIEWS):
        dz = shift_of(taps, v)

        @pl.when(dz < 0)
        def _(v=v, n=n_up):
            up[pl.ds(pl.multiple_of(n * FLAT, FLAT), FLAT)] = held[v]

        @pl.when(dz > 0)
        def _(v=v, n=n_down):
            down[pl.ds(pl.multiple_of(n * FLAT, FLAT), FLAT)] = held[v]

        n_up = n_up + jnp.where(dz < 0, 1, 0)
        n_down = n_down + jnp.where(dz > 0, 1, 0)


def bands_body(taps, wy_f, wy_b, wx_f, wx_b):
    dims = (ROWS, 4 * EXT)
    lane = iota(dims, 1)
    gap = (lane & (EXT - 1)) - iota(dims, 0) - 1
    for v in range(VIEWS):
        band = jnp.zeros(dims, F32)
        for a in range(TAPS):
            band = jnp.where(gap == a, taps[v, HY, a], band)
        high = band.astype(BF16).astype(F32)
        wy_f[v * ROWS : (v + 1) * ROWS, :] = jnp.where(lane < 2 * EXT, high, band - high).astype(BF16)

    dims = (EXT, LANES)
    lane = iota(dims, 1)
    gap = iota(dims, 0) - (lane & (ROWS - 1)) - 1
    band = jnp.zeros(dims, F32)
    for a in range(TAPS):
        tap = jnp.zeros((1, LANES), F32)
        for v in range(VIEWS):
            tap = jnp.where(iota((1, LANES), 1) >= v * ROWS, taps[v, HY, a], tap)
        band = jnp.where(gap == a, tap, band)
    high, low = pieces(band)
    wy_b[...] = jnp.concatenate([jnp.concatenate([high, high], 1), jnp.concatenate([low, low], 1)], 0)

    dims = (LANES, LANES)
    gap = iota(dims, 0) - iota(dims, 1)
    for v in range(VIEWS):
        for out, sign in ((wx_f, 1), (wx_b, -1)):
            band = jnp.zeros(dims, F32)
            for a in range(TAPS):
                band = jnp.where(gap == sign * (a - HALF), taps[v, HX, a], band)
            high, low = pieces(band)
            part = jnp.concatenate([high, low], 1)
            out[v] = jnp.concatenate([part, part], 0)


def forward_body(taps, before, own, after, wy_f, wx_f, out, inner, summed):
    _, _, block = position()

    def layer(k):
        if k < HALF:
            return jnp.where(block > 0, before[k + 1], 0.0)
        if k < HALF + BZ:
            return own[k - HALF]
        return jnp.where(block < 63, after[k - HALF - BZ], 0.0)

    for p in range(LAYERS // 2):
        high, low = pieces(jnp.concatenate([layer(2 * p), layer(2 * p + 1)], 1))
        data = jnp.concatenate([high, low, high, low], 0)
        done = jnp.dot(wy_f[...], data, preferred_element_type=F32)
        for v in range(VIEWS):
            rows = done[v * ROWS : (v + 1) * ROWS]
            inner[v, 2 * p] = rows[:, :LANES]
            inner[v, 2 * p + 1] = rows[:, LANES:]

    def sum_z(v):
        hz = [taps[v, HZ, a] for a in range(TAPS)]
        for t in range(ROWS // 8):
            rows = slice(8 * t, 8 * t + 8)
            acc = [None] * BZ
            for k in range(LAYERS):
                x = inner[v, k, rows, :]
                for i in range(max(0, k - TAPS + 1), min(BZ - 1, k) + 1):
                    term = hz[k - i] * x
                    acc[i] = term if acc[i] is None else acc[i] + term
            for i in range(BZ):
                summed[v, i, rows, :] = acc[i]

    def mix_x(v):
        high, low = pieces(summed[v].reshape(BZ * ROWS, LANES))
        done = jnp.dot(jnp.concatenate([high, low], 1), wx_f[v], preferred_element_type=F32)
        out[v] = (done[:, :LANES] + done[:, LANES:]).reshape(BZ, ROWS, LANES)

    for v in range(VIEWS):
        sum_z(v)
        if v > 0:
            mix_x(v - 1)
    mix_x(VIEWS - 1)


def back_body(taps, fwd, rec, wx_b, wy_b, before, own, after, inner, spread_z):
    def mix_x(v):
        ratio = (rec[v] / fwd[v]).reshape(BZ * ROWS, LANES)
        high, low = pieces(ratio)
        done = jnp.dot(jnp.concatenate([high, low], 1), wx_b[v], preferred_element_type=F32)
        inner[v] = (done[:, :LANES] + done[:, LANES:]).reshape(BZ, ROWS, LANES)

    def spread_layers(v):
        hz = [taps[v, WZ, a] for a in range(TAPS)]
        for t in range(ROWS // 8):
            x = [inner[v, i, 8 * t : 8 * t + 8, :] for i in range(BZ)]
            for k in range(LAYERS):
                acc = None
                for i in range(max(0, k - TAPS + 1), min(BZ - 1, k) + 1):
                    term = hz[k - i] * x[i]
                    acc = term if acc is None else acc + term
                spread_z[k, v * ROWS + 8 * t : v * ROWS + 8 * t + 8, :] = acc

    mix_x(0)
    for v in range(VIEWS):
        if v < VIEWS - 1:
            mix_x(v + 1)
        spread_layers(v)

    def store(k, value):
        if k < HALF:
            before[k] = value
        elif k < HALF + BZ:
            own[k - HALF] = value
        else:
            after[k - HALF - BZ] = value

    for p in range(LAYERS // 2):
        high, low = pieces(jnp.concatenate([spread_z[2 * p], spread_z[2 * p + 1]], 1))
        done = jnp.dot(wy_b[...], jnp.concatenate([high, low], 0), preferred_element_type=F32)
        both = done[:EXT] + done[EXT:]
        store(2 * p, both[:, :LANES])
        store(2 * p + 1, both[:, LANES:])


def first_back_body(taps, fwd, a0, a1, a2, a3, lower, upper, wx_b, wy_b, *rest):
    before, own, after, rec, held, low, high, sems, inner, spread_z = rest
    _, _, block = position()
    copies = [pltpu.make_async_copy(lower, low, sems.at[4]), pltpu.make_async_copy(upper, high, sems.at[5])]
    for j, a in enumerate((a0, a1, a2, a3)):
        copies.append(pltpu.make_async_copy(a.at[pl.ds(0, FLAT)], held.at[view_at(j)], sems.at[j]))
    for copy in copies:
        copy.start()
    for copy in copies:
        copy.wait()
    n_up, n_down = jnp.int32(0), jnp.int32(0)
    for v in range(VIEWS):
        dz = shift_of(taps, v)

        @pl.loop(0, BZ)
        def _(i, v=v, dz=dz, n_up=n_up, n_down=n_down):
            src = i + dz
            place_z = block * BZ + src

            def rows(layer, count):
                return pl.ds(pl.multiple_of(jnp.clip(layer, 0, count - 1) * ROWS, ROWS), ROWS)

            x = held[v, rows(src, BZ), :]
            x = jnp.where(src < 0, low[rows(n_up * BZ + src + BZ, 3 * BZ), :], x)
            x = jnp.where(src >= BZ, high[rows(n_down * BZ + src - BZ, 3 * BZ), :], x)
            rec[v, i] = jnp.where((place_z >= 0) & (place_z < 64 * BZ), x, 0.0)

        n_up = n_up + jnp.where(dz < 0, 1, 0)
        n_down = n_down + jnp.where(dz > 0, 1, 0)

    back_body(taps, fwd, rec, wx_b, wy_b, before, own, after, inner, spread_z)


def add_layers(own, from_prev, from_next, cut):
    _, _, block = position()
    out = []
    for i in range(BZ):
        value = own[i, cut]
        if i < HALF:
            value = value + jnp.where(block > 0, from_prev[i, cut], 0.0)
        if i > 0:
            value = value + jnp.where(block < 63, from_next[i - 1, cut], 0.0)
        out.append(value)
    return out


def halves_body(own, from_prev, from_next, low, high):
    for out, cut in ((low, slice(0, ROWS)), (high, slice(ROWS, EXT))):
        for i, value in enumerate(add_layers(own, from_prev, from_next, cut)):
            out[i] = value


def edges_body(own, from_prev, from_next, low, middle, high):
    cuts = (slice(0, EDGE), slice(EDGE, EXT - EDGE), slice(EXT - EDGE, EXT))
    for out, cut in zip((low, middle, high), cuts):
        for i, value in enumerate(add_layers(own, from_prev, from_next, cut)):
            out[i] = value


def view_sum(taps):
    return taps[0, MISC, 0] + taps[1, MISC, 0] + taps[2, MISC, 0] + taps[3, MISC, 0]


def window_body(taps, ext, low, high, from_prev, from_next, out):
    _, r, _ = position()
    wsum = view_sum(taps)
    for i in range(BZ):
        total = low[i] + jnp.where(r > 0, from_prev[i], 0.0)
        out[i, :ROWS] = ext[i, :ROWS] * total / wsum
        total = high[i] + jnp.where(r < 3, from_next[i], 0.0)
        out[i, ROWS:] = ext[i, ROWS:] * total / wsum


def last_body(taps, ext, middle, from_prev, from_next, out):
    _, r, _ = position()
    wsum = view_sum(taps)
    for i in range(BZ):
        total = middle[i, :EDGE] + jnp.where(r > 0, from_prev[i], 0.0)
        out[i, :EDGE] = ext[i, EDGE:ROWS] * total / wsum
        total = middle[i, EDGE:] + jnp.where(r < 3, from_next[i], 0.0)
        out[i, EDGE:] = ext[i, ROWS : EXT - EDGE] * total / wsum


def join_body(c0, c1, c2, c3, out):
    for mask, chunk in enumerate((c0, c1, c2, c3)):
        start = pl.multiple_of(quarter_at(mask) * ROWS, ROWS)
        out[:, pl.ds(start, ROWS), :] = chunk[...]


BLOCK = (VIEWS, BZ, ROWS, LANES)
INNER = (VIEWS, LAYERS, ROWS, LANES)
SPREAD = (LAYERS, LANES, LANES)
WINDOW = (BZ, EXT, LANES)
HALO = (HALF, EXT, LANES)
QUARTER = (BZ, ROWS, LANES)
PACKED = (3 * FLAT, LANES)
STRIP = (BZ, EDGE, LANES)


def per_device(estimate, recorded, offsets, psf_z, psf_y, psf_x, view_weights):
    with jax.named_scope("window"):
        ext = call(start_body, shape(*WINDOW), (estimate,), [hbm()], [pltpu.SemaphoreType.DMA], 1_000_000)
        ext = spread(ext, 0)
    with jax.named_scope("planes"):
        chunks = call(
            planes_body,
            (shape(FLAT + 8, LANES),) * 4,
            (offsets, view_weights, recorded, psf_z, psf_y, psf_x),
            [smem(), smem()] + [vmem()] * 4,
            [pltpu.VMEM((BZ, LANES, LANES), F32)],
            10_000_000,
        )
    with jax.named_scope("spread"):
        mine = [spread(c, j) for j, c in enumerate(chunks)]
    with jax.named_scope("layers_in"):
        before = to_layer(ext, 1)
        after = to_layer(ext, -1)
    with jax.named_scope("shift"):
        up, down, taps = call(
            pack_body,
            (shape(*PACKED), shape(*PACKED), shape(VIEWS, 8, LANES)),
            tuple(mine),
            [hbm()] * 4,
            [pltpu.VMEM((VIEWS, FLAT, LANES), F32), pltpu.SemaphoreType.DMA((4,)), pltpu.SemaphoreType.DMA((4,))],
            8_000_000_000,
            (vmem(), vmem(), smem()),
        )
        lower = to_layer(up, 1)
        upper = to_layer(down, -1)

    with jax.named_scope("bands"):
        wy_f, wy_b, wx_f, wx_b = call(
            bands_body,
            (
                shape(LANES, 4 * EXT, dtype=BF16),
                shape(LANES, 2 * LANES, dtype=BF16),
                shape(VIEWS, 2 * LANES, 2 * LANES, dtype=BF16),
                shape(VIEWS, 2 * LANES, 2 * LANES, dtype=BF16),
            ),
            (taps,),
            [smem()],
            [],
            30_000_000,
        )

    rec = None
    for step in range(ITERS):
        if step > 0:
            with jax.named_scope("layers_in"):
                before = to_layer(ext, 1)
                after = to_layer(ext, -1)
        with jax.named_scope("forward"):
            fwd = call(
                forward_body,
                shape(*BLOCK),
                (taps, before, ext, after, wy_f, wx_f),
                [smem()] + [vmem()] * 5,
                [pltpu.VMEM(INNER, F32), pltpu.VMEM(BLOCK, F32)],
                20_000_000_000 if step == 0 else 2_000_000_000,
            )
        with jax.named_scope("back"):
            outs = (shape(*HALO), shape(*WINDOW), shape(*HALO))
            scratch = [pltpu.VMEM(BLOCK, F32), pltpu.VMEM(SPREAD, F32)]
            if rec is None:
                c_before, c_own, c_after, rec = call(
                    first_back_body,
                    outs + (shape(*BLOCK),),
                    (taps, fwd, *mine, lower, upper, wx_b, wy_b),
                    [smem(), vmem()] + [hbm()] * 6 + [vmem()] * 2,
                    [
                        pltpu.VMEM((VIEWS, FLAT, LANES), F32),
                        pltpu.VMEM(PACKED, F32),
                        pltpu.VMEM(PACKED, F32),
                        pltpu.SemaphoreType.DMA((6,)),
                    ]
                    + scratch,
                    2_000_000_000,
                )
            else:
                c_before, c_own, c_after = call(
                    back_body,
                    outs,
                    (taps, fwd, rec, wx_b, wy_b),
                    [smem()] + [vmem()] * 4,
                    scratch,
                    2_000_000_000,
                )
        with jax.named_scope("layers_out"):
            from_next = to_layer(c_before, -1)
            from_prev = to_layer(c_after, 1)
        if step < ITERS - 1:
            with jax.named_scope("rows"):
                low, high = call(
                    halves_body, (shape(*QUARTER),) * 2, (c_own, from_prev, from_next), [vmem()] * 3, [], 1_000_000
                )
                row_prev = to_row(high, 1)
                row_next = to_row(low, -1)
                ext = call(
                    window_body,
                    shape(*WINDOW),
                    (taps, ext, low, high, row_prev, row_next),
                    [smem()] + [vmem()] * 5,
                    [],
                    1_000_000,
                )
        else:
            with jax.named_scope("rows"):
                low, middle, high = call(
                    edges_body,
                    (shape(*STRIP), shape(*QUARTER), shape(*STRIP)),
                    (c_own, from_prev, from_next),
                    [vmem()] * 3,
                    [],
                    1_000_000,
                )
                row_prev = to_row(high, 1)
                row_next = to_row(low, -1)
                own = call(
                    last_body,
                    shape(*QUARTER),
                    (taps, ext, middle, row_prev, row_next),
                    [smem()] + [vmem()] * 4,
                    [],
                    1_000_000,
                )

    with jax.named_scope("result"):
        c0 = collect(own, 0)
        c1 = view_swap(c0, 1)
        c2 = collect(own, 2)
        c3 = view_swap(c2, 1)
        return call(join_body, shape(BZ, LANES, LANES), (c0, c1, c2, c3), [vmem()] * 4, [], 1_000_000)


def solution(mesh):
    in_specs = (
        P("blk", None, None),
        P("view", "blk", None, None),
        P("view", None),
        P("view", None),
        P("view", None),
        P("view", None),
        P("view"),
    )
    out_specs = P("blk", None, None)
    return jax.shard_map(
        per_device, mesh=mesh, in_specs=in_specs, out_specs=out_specs, check_vma=False
    )
```

```python
import jax
import jax.numpy as jnp
from jax import lax
from jax.experimental import pallas as pl
from jax.experimental.pallas import tpu as pltpu
from jax.sharding import PartitionSpec as P

ITERS = 2
TAPS = 31
HALF = 15
VIEWS = 4
BZ = 16
ROWS = 32
FLAT = BZ * ROWS
EXT = 64
LANES = 128
EDGE = 16
LAYERS = BZ + 2 * HALF
AXES = ("blk", "view")
HZ, HY, HX, WZ, MISC = 0, 1, 2, 3, 4
F32 = jnp.float32
BF16 = jnp.bfloat16

CELLS = [(z, y, x, v) for z in range(4) for y in range(4) for x in range(4) for v in range(4)]


def device(z, y, x, v):
    return ((z * 4 + y) * 4 + x) * 4 + v


PATH = ((0, 0), (1, 0), (1, 1), (2, 1), (2, 0), (3, 0), (3, 1), (0, 1))


def place(block, r):
    z, chip, core = block // 16, (block // 2) % 8, block % 2
    y, z_lo = PATH[chip]
    return device(z, y, r, 2 * z_lo + (core ^ (chip % 2)))


FAR = (1, 3, 0, 2)


def quarter_of(q, v, j):
    return (q + FAR[v ^ j]) % 4


def spread(x, j):
    perm = [(device(z, y, q, v), place(16 * z + 4 * y + q, quarter_of(q, v, j))) for z, y, q, v in CELLS]
    return lax.ppermute(x, AXES, perm)


def collect(x, j):
    perm = [(place(16 * z + 4 * y + q, quarter_of(q, v, j)), device(z, y, q, v)) for z, y, q, v in CELLS]
    return lax.ppermute(x, AXES, perm)


def view_swap(x, mask):
    return lax.ppermute(x, AXES, [(device(z, y, c, v), device(z, y, c, v ^ mask)) for z, y, c, v in CELLS])


def to_layer(x, step):
    perm = [(place(b, r), place((b + step) % 64, r)) for b in range(64) for r in range(4)]
    return lax.ppermute(x, AXES, perm)


def to_row(x, step):
    perm = [(place(b, r), place(b, (r + step) % 4)) for b in range(64) for r in range(4)]
    return lax.ppermute(x, AXES, perm)


def position():
    blk, view = lax.axis_index("blk"), lax.axis_index("view")
    y = lax.rem(lax.div(blk, 4), 4)
    near = jnp.where(y < 2, y, y + 2)
    far = jnp.where(y == 0, 7, jnp.where(y == 3, 6, y + 1))
    chip = jnp.where(view < 2, near, far)
    core = (view & 1) ^ (chip & 1)
    return view, lax.rem(blk, 4), lax.div(blk, 16) * 16 + 2 * chip + core


def quarter_at(j):
    q = lax.rem(lax.axis_index("blk"), 4)
    slot = lax.axis_index("view") ^ j
    far = jnp.where(slot == 0, 1, jnp.where(slot == 1, 3, jnp.where(slot == 2, 0, 2)))
    return lax.rem(q + far, 4)


def view_at(j):
    _, r, block = position()
    far = lax.rem(r - lax.rem(block, 4) + 4, 4)
    return jnp.where(far == 1, 0, jnp.where(far == 3, 1, jnp.where(far == 0, 2, 3))) ^ j


def vmem():
    return pl.BlockSpec(memory_space=pltpu.VMEM)


def smem():
    return pl.BlockSpec(memory_space=pltpu.SMEM)


def hbm():
    return pl.BlockSpec(memory_space=pl.ANY)


def call(body, outs, args, specs, scratch, flops, out_specs=None, mib=48):
    size = sum(a.size * a.dtype.itemsize for a in args)
    return pl.pallas_call(
        body,
        out_shape=outs,
        in_specs=specs,
        out_specs=out_specs or jax.tree.map(lambda _: vmem(), outs),
        scratch_shapes=scratch,
        compiler_params=pltpu.CompilerParams(vmem_limit_bytes=mib * 1024 * 1024),
        cost_estimate=pl.CostEstimate(flops=flops, bytes_accessed=size, transcendentals=0),
    )(*args)


def shape(*dims, dtype=F32):
    return jax.ShapeDtypeStruct(dims, dtype)


def iota(dims, axis):
    return lax.broadcasted_iota(jnp.int32, dims, axis)


def pieces(x):
    high = x.astype(BF16)
    low = (x - high.astype(F32)).astype(BF16)
    return high, low


def start_body(est, ext, sem):
    def window(k):
        first = max(0, k * ROWS - EDGE)
        size = min(LANES, (k + 1) * ROWS + EDGE) - first
        skip = first - (k * ROWS - EDGE)
        return pltpu.make_async_copy(est.at[:, pl.ds(first, size)], ext.at[:, pl.ds(skip, size)], sem)

    for k in range(VIEWS):

        @pl.when(quarter_at(0) == k)
        def _(k=k):
            window(k).start()
            if k == 0:
                ext[:, :EDGE, :] = jnp.zeros((BZ, EDGE, LANES), F32)
            if k == VIEWS - 1:
                ext[:, EXT - EDGE :, :] = jnp.zeros((BZ, EDGE, LANES), F32)
            window(k).wait()


def planes_body(offsets, weight, rec, psf_z, psf_y, psf_x, o0, o1, o2, o3, moved):
    dy, dx = offsets[0, 1], offsets[0, 2]
    row = iota((LANES, LANES), 0) + dy
    col = iota((LANES, LANES), 1) + dx
    inside = (row >= 0) & (row < LANES) & (col >= 0) & (col < LANES)
    back_y = lax.rem(LANES - dy, LANES)
    back_x = lax.rem(LANES - dx, LANES)

    @pl.loop(0, BZ, unroll=4)
    def _(z):
        plane = pltpu.roll(pltpu.roll(rec[0, z], back_y, 0), back_x, 1)
        moved[z] = jnp.where(inside, plane, 0.0)

    hz, hy, hx = (t[...] / jnp.sum(t[...], axis=1, keepdims=True) for t in (psf_z, psf_y, psf_x))
    lane = iota((1, LANES), 1)
    misc = jnp.where(lane == 0, weight[0], jnp.where(lane == 1, offsets[0, 0].astype(F32), 0.0))
    for j, out in enumerate((o0, o1, o2, o3)):
        start = pl.multiple_of(quarter_at(j) * ROWS, ROWS)
        out[:FLAT] = moved[:, pl.ds(start, ROWS), :].reshape(FLAT, LANES)
        out[FLAT:] = jnp.zeros((8, LANES), F32)
        for row, value in ((HZ, hz), (HY, hy), (HX, hx), (WZ, weight[0] * hz)):
            out[FLAT + row : FLAT + row + 1, :TAPS] = value
        out[FLAT + MISC : FLAT + MISC + 1, :] = misc


def shift_of(taps, v):
    return taps[v, MISC, 1].astype(jnp.int32)


def pack_body(a0, a1, a2, a3, up, down, taps, held, sems, tap_sems):
    blocks = (a0, a1, a2, a3)
    data, rows = [], []
    for j, a in enumerate(blocks):
        data.append(pltpu.make_async_copy(a.at[pl.ds(0, FLAT)], held.at[view_at(j)], sems.at[j]))
        rows.append(pltpu.make_async_copy(a.at[pl.ds(FLAT, 8)], taps.at[view_at(j)], tap_sems.at[j]))
    for copy in rows + data:
        copy.start()
    for copy in rows + data:
        copy.wait()
    for out in (up, down):
        out[FLAT:] = jnp.zeros((2 * FLAT, LANES), F32)
    n_up, n_down = jnp.int32(0), jnp.int32(0)
    for v in range(VIEWS):
        dz = shift_of(taps, v)

        @pl.when(dz < 0)
        def _(v=v, n=n_up):
            up[pl.ds(pl.multiple_of(n * FLAT, FLAT), FLAT)] = held[v]

        @pl.when(dz > 0)
        def _(v=v, n=n_down):
            down[pl.ds(pl.multiple_of(n * FLAT, FLAT), FLAT)] = held[v]

        n_up = n_up + jnp.where(dz < 0, 1, 0)
        n_down = n_down + jnp.where(dz > 0, 1, 0)


def bands_body(taps, wy_f, wy_b, wx_f, wx_b):
    dims = (ROWS, 4 * EXT)
    lane = iota(dims, 1)
    gap = (lane & (EXT - 1)) - iota(dims, 0) - 1
    for v in range(VIEWS):
        band = jnp.zeros(dims, F32)
        for a in range(TAPS):
            band = jnp.where(gap == a, taps[v, HY, a], band)
        high = band.astype(BF16).astype(F32)
        wy_f[v * ROWS : (v + 1) * ROWS, :] = jnp.where(lane < 2 * EXT, high, band - high).astype(BF16)

    dims = (EXT, LANES)
    lane = iota(dims, 1)
    gap = iota(dims, 0) - (lane & (ROWS - 1)) - 1
    band = jnp.zeros(dims, F32)
    for a in range(TAPS):
        tap = jnp.zeros((1, LANES), F32)
        for v in range(VIEWS):
            tap = jnp.where(iota((1, LANES), 1) >= v * ROWS, taps[v, HY, a], tap)
        band = jnp.where(gap == a, tap, band)
    high, low = pieces(band)
    wy_b[...] = jnp.concatenate([jnp.concatenate([high, high], 1), jnp.concatenate([low, low], 1)], 0)

    dims = (LANES, LANES)
    gap = iota(dims, 0) - iota(dims, 1)
    for v in range(VIEWS):
        for out, sign in ((wx_f, 1), (wx_b, -1)):
            band = jnp.zeros(dims, F32)
            for a in range(TAPS):
                band = jnp.where(gap == sign * (a - HALF), taps[v, HX, a], band)
            high, low = pieces(band)
            part = jnp.concatenate([high, low], 1)
            out[v] = jnp.concatenate([part, part], 0)


def forward_body(taps, before, own, after, wy_f, wx_f, out, inner, summed):
    _, _, block = position()

    def layer(k):
        if k < HALF:
            return jnp.where(block > 0, before[k + 1], 0.0)
        if k < HALF + BZ:
            return own[k - HALF]
        return jnp.where(block < 63, after[k - HALF - BZ], 0.0)

    for p in range(LAYERS // 2):
        high, low = pieces(jnp.concatenate([layer(2 * p), layer(2 * p + 1)], 1))
        data = jnp.concatenate([high, low, high, low], 0)
        done = jnp.dot(wy_f[...], data, preferred_element_type=F32)
        for v in range(VIEWS):
            rows = done[v * ROWS : (v + 1) * ROWS]
            inner[v, 2 * p] = rows[:, :LANES]
            inner[v, 2 * p + 1] = rows[:, LANES:]

    def sum_z(v):
        hz = [taps[v, HZ, a] for a in range(TAPS)]
        for t in range(ROWS // 8):
            rows = slice(8 * t, 8 * t + 8)
            acc = [None] * BZ
            for k in range(LAYERS):
                x = inner[v, k, rows, :]
                for i in range(max(0, k - TAPS + 1), min(BZ - 1, k) + 1):
                    term = hz[k - i] * x
                    acc[i] = term if acc[i] is None else acc[i] + term
            for i in range(BZ):
                summed[v, i, rows, :] = acc[i]

    def mix_x(v):
        high, low = pieces(summed[v].reshape(BZ * ROWS, LANES))
        done = jnp.dot(jnp.concatenate([high, low], 1), wx_f[v], preferred_element_type=F32)
        out[v] = (done[:, :LANES] + done[:, LANES:]).reshape(BZ, ROWS, LANES)

    for v in range(VIEWS):
        sum_z(v)
        if v > 0:
            mix_x(v - 1)
    mix_x(VIEWS - 1)


def back_body(taps, fwd, rec, wx_b, wy_b, before, own, after, inner, spread_z):
    def mix_x(v):
        ratio = (rec[v] / fwd[v]).reshape(BZ * ROWS, LANES)
        high, low = pieces(ratio)
        done = jnp.dot(jnp.concatenate([high, low], 1), wx_b[v], preferred_element_type=F32)
        inner[v] = (done[:, :LANES] + done[:, LANES:]).reshape(BZ, ROWS, LANES)

    def spread_layers(v):
        hz = [taps[v, WZ, a] for a in range(TAPS)]
        for t in range(ROWS // 8):
            x = [inner[v, i, 8 * t : 8 * t + 8, :] for i in range(BZ)]
            for k in range(LAYERS):
                acc = None
                for i in range(max(0, k - TAPS + 1), min(BZ - 1, k) + 1):
                    term = hz[k - i] * x[i]
                    acc = term if acc is None else acc + term
                spread_z[k, v * ROWS + 8 * t : v * ROWS + 8 * t + 8, :] = acc

    mix_x(0)
    for v in range(VIEWS):
        if v < VIEWS - 1:
            mix_x(v + 1)
        spread_layers(v)

    def store(k, value):
        if k < HALF:
            before[k] = value
        elif k < HALF + BZ:
            own[k - HALF] = value
        else:
            after[k - HALF - BZ] = value

    for p in range(LAYERS // 2):
        high, low = pieces(jnp.concatenate([spread_z[2 * p], spread_z[2 * p + 1]], 1))
        done = jnp.dot(wy_b[...], jnp.concatenate([high, low], 0), preferred_element_type=F32)
        both = done[:EXT] + done[EXT:]
        store(2 * p, both[:, :LANES])
        store(2 * p + 1, both[:, LANES:])


def first_back_body(taps, fwd, a0, a1, a2, a3, lower, upper, wx_b, wy_b, *rest):
    before, own, after, rec, held, low, high, sems, inner, spread_z = rest
    _, _, block = position()
    copies = [pltpu.make_async_copy(lower, low, sems.at[4]), pltpu.make_async_copy(upper, high, sems.at[5])]
    for j, a in enumerate((a0, a1, a2, a3)):
        copies.append(pltpu.make_async_copy(a.at[pl.ds(0, FLAT)], held.at[view_at(j)], sems.at[j]))
    for copy in copies:
        copy.start()
    for copy in copies:
        copy.wait()
    n_up, n_down = jnp.int32(0), jnp.int32(0)
    for v in range(VIEWS):
        dz = shift_of(taps, v)

        @pl.loop(0, BZ, unroll=8)
        def _(i, v=v, dz=dz, n_up=n_up, n_down=n_down):
            src = i + dz
            place_z = block * BZ + src

            def rows(layer, count):
                return pl.ds(pl.multiple_of(jnp.clip(layer, 0, count - 1) * ROWS, ROWS), ROWS)

            x = held[v, rows(src, BZ), :]
            x = jnp.where(src < 0, low[rows(n_up * BZ + src + BZ, 3 * BZ), :], x)
            x = jnp.where(src >= BZ, high[rows(n_down * BZ + src - BZ, 3 * BZ), :], x)
            rec[v, i] = jnp.where((place_z >= 0) & (place_z < 64 * BZ), x, 0.0)

        n_up = n_up + jnp.where(dz < 0, 1, 0)
        n_down = n_down + jnp.where(dz > 0, 1, 0)

    back_body(taps, fwd, rec, wx_b, wy_b, before, own, after, inner, spread_z)


def add_layers(own, from_prev, from_next, cut):
    _, _, block = position()
    out = []
    for i in range(BZ):
        value = own[i, cut]
        if i < HALF:
            value = value + jnp.where(block > 0, from_prev[i, cut], 0.0)
        if i > 0:
            value = value + jnp.where(block < 63, from_next[i - 1, cut], 0.0)
        out.append(value)
    return out


def halves_body(own, from_prev, from_next, low, high):
    for out, cut in ((low, slice(0, ROWS)), (high, slice(ROWS, EXT))):
        for i, value in enumerate(add_layers(own, from_prev, from_next, cut)):
            out[i] = value


def edges_body(own, from_prev, from_next, low, middle, high):
    cuts = (slice(0, EDGE), slice(EDGE, EXT - EDGE), slice(EXT - EDGE, EXT))
    for out, cut in zip((low, middle, high), cuts):
        for i, value in enumerate(add_layers(own, from_prev, from_next, cut)):
            out[i] = value


def view_sum(taps):
    return taps[0, MISC, 0] + taps[1, MISC, 0] + taps[2, MISC, 0] + taps[3, MISC, 0]


def window_body(taps, ext, low, high, from_prev, from_next, out):
    _, r, _ = position()
    wsum = view_sum(taps)
    for i in range(BZ):
        total = low[i] + jnp.where(r > 0, from_prev[i], 0.0)
        out[i, :ROWS] = ext[i, :ROWS] * total / wsum
        total = high[i] + jnp.where(r < 3, from_next[i], 0.0)
        out[i, ROWS:] = ext[i, ROWS:] * total / wsum


def last_body(taps, ext, middle, from_prev, from_next, out):
    _, r, _ = position()
    wsum = view_sum(taps)
    for i in range(BZ):
        total = middle[i, :EDGE] + jnp.where(r > 0, from_prev[i], 0.0)
        out[i, :EDGE] = ext[i, EDGE:ROWS] * total / wsum
        total = middle[i, EDGE:] + jnp.where(r < 3, from_next[i], 0.0)
        out[i, EDGE:] = ext[i, ROWS : EXT - EDGE] * total / wsum


def join_body(c0, c1, c2, c3, out):
    for mask, chunk in enumerate((c0, c1, c2, c3)):
        start = pl.multiple_of(quarter_at(mask) * ROWS, ROWS)
        out[:, pl.ds(start, ROWS), :] = chunk[...]


BLOCK = (VIEWS, BZ, ROWS, LANES)
INNER = (VIEWS, LAYERS, ROWS, LANES)
SPREAD = (LAYERS, LANES, LANES)
WINDOW = (BZ, EXT, LANES)
HALO = (HALF, EXT, LANES)
QUARTER = (BZ, ROWS, LANES)
PACKED = (3 * FLAT, LANES)
STRIP = (BZ, EDGE, LANES)


def per_device(estimate, recorded, offsets, psf_z, psf_y, psf_x, view_weights):
    with jax.named_scope("window"):
        ext = call(start_body, shape(*WINDOW), (estimate,), [hbm()], [pltpu.SemaphoreType.DMA], 1_000_000)
        ext = spread(ext, 0)
    with jax.named_scope("planes"):
        chunks = call(
            planes_body,
            (shape(FLAT + 8, LANES),) * 4,
            (offsets, view_weights, recorded, psf_z, psf_y, psf_x),
            [smem(), smem()] + [vmem()] * 4,
            [pltpu.VMEM((BZ, LANES, LANES), F32)],
            10_000_000,
        )
    with jax.named_scope("spread"):
        mine = [spread(c, j) for j, c in enumerate(chunks)]
    with jax.named_scope("layers_in"):
        before = to_layer(ext, 1)
        after = to_layer(ext, -1)
    with jax.named_scope("shift"):
        up, down, taps = call(
            pack_body,
            (shape(*PACKED), shape(*PACKED), shape(VIEWS, 8, LANES)),
            tuple(mine),
            [hbm()] * 4,
            [pltpu.VMEM((VIEWS, FLAT, LANES), F32), pltpu.SemaphoreType.DMA((4,)), pltpu.SemaphoreType.DMA((4,))],
            8_000_000_000,
            (vmem(), vmem(), smem()),
        )
        lower = to_layer(up, 1)
        upper = to_layer(down, -1)

    with jax.named_scope("bands"):
        wy_f, wy_b, wx_f, wx_b = call(
            bands_body,
            (
                shape(LANES, 4 * EXT, dtype=BF16),
                shape(LANES, 2 * LANES, dtype=BF16),
                shape(VIEWS, 2 * LANES, 2 * LANES, dtype=BF16),
                shape(VIEWS, 2 * LANES, 2 * LANES, dtype=BF16),
            ),
            (taps,),
            [smem()],
            [],
            30_000_000,
        )

    rec = None
    for step in range(ITERS):
        if step > 0:
            with jax.named_scope("layers_in"):
                before = to_layer(ext, 1)
                after = to_layer(ext, -1)
        with jax.named_scope("forward"):
            fwd = call(
                forward_body,
                shape(*BLOCK),
                (taps, before, ext, after, wy_f, wx_f),
                [smem()] + [vmem()] * 5,
                [pltpu.VMEM(INNER, F32), pltpu.VMEM(BLOCK, F32)],
                20_000_000_000 if step == 0 else 2_000_000_000,
            )
        with jax.named_scope("back"):
            outs = (shape(*HALO), shape(*WINDOW), shape(*HALO))
            scratch = [pltpu.VMEM(BLOCK, F32), pltpu.VMEM(SPREAD, F32)]
            if rec is None:
                c_before, c_own, c_after, rec = call(
                    first_back_body,
                    outs + (shape(*BLOCK),),
                    (taps, fwd, *mine, lower, upper, wx_b, wy_b),
                    [smem(), vmem()] + [hbm()] * 6 + [vmem()] * 2,
                    [
                        pltpu.VMEM((VIEWS, FLAT, LANES), F32),
                        pltpu.VMEM(PACKED, F32),
                        pltpu.VMEM(PACKED, F32),
                        pltpu.SemaphoreType.DMA((6,)),
                    ]
                    + scratch,
                    2_000_000_000,
                )
            else:
                c_before, c_own, c_after = call(
                    back_body,
                    outs,
                    (taps, fwd, rec, wx_b, wy_b),
                    [smem()] + [vmem()] * 4,
                    scratch,
                    2_000_000_000,
                )
        with jax.named_scope("layers_out"):
            from_next = to_layer(c_before, -1)
            from_prev = to_layer(c_after, 1)
        if step < ITERS - 1:
            with jax.named_scope("rows"):
                low, high = call(
                    halves_body, (shape(*QUARTER),) * 2, (c_own, from_prev, from_next), [vmem()] * 3, [], 1_000_000
                )
                row_prev = to_row(high, 1)
                row_next = to_row(low, -1)
                ext = call(
                    window_body,
                    shape(*WINDOW),
                    (taps, ext, low, high, row_prev, row_next),
                    [smem()] + [vmem()] * 5,
                    [],
                    1_000_000,
                )
        else:
            with jax.named_scope("rows"):
                low, middle, high = call(
                    edges_body,
                    (shape(*STRIP), shape(*QUARTER), shape(*STRIP)),
                    (c_own, from_prev, from_next),
                    [vmem()] * 3,
                    [],
                    1_000_000,
                )
                row_prev = to_row(high, 1)
                row_next = to_row(low, -1)
                own = call(
                    last_body,
                    shape(*QUARTER),
                    (taps, ext, middle, row_prev, row_next),
                    [smem()] + [vmem()] * 4,
                    [],
                    1_000_000,
                )

    with jax.named_scope("result"):
        c0 = collect(own, 0)
        c1 = view_swap(c0, 1)
        c2 = collect(own, 2)
        c3 = view_swap(c2, 1)
        return call(join_body, shape(BZ, LANES, LANES), (c0, c1, c2, c3), [vmem()] * 4, [], 1_000_000)


def solution(mesh):
    in_specs = (
        P("blk", None, None),
        P("view", "blk", None, None),
        P("view", None),
        P("view", None),
        P("view", None),
        P("view", None),
        P("view"),
    )
    out_specs = P("blk", None, None)
    return jax.shard_map(
        per_device, mesh=mesh, in_specs=in_specs, out_specs=out_specs, check_vma=False
    )
```

```python
import jax
import jax.numpy as jnp
from jax import lax
from jax.experimental import pallas as pl
from jax.experimental.pallas import tpu as pltpu
from jax.sharding import PartitionSpec as P

ITERS = 2
TAPS = 31
HALF = 15
VIEWS = 4
BZ = 16
ROWS = 32
FLAT = BZ * ROWS
EXT = 64
LANES = 128
EDGE = 16
LAYERS = BZ + 2 * HALF
AXES = ("blk", "view")
HZ, HY, HX, WZ, MISC = 0, 1, 2, 3, 4
F32 = jnp.float32
BF16 = jnp.bfloat16

CELLS = [(z, y, x, v) for z in range(4) for y in range(4) for x in range(4) for v in range(4)]


def device(z, y, x, v):
    return ((z * 4 + y) * 4 + x) * 4 + v


PATH = ((0, 0), (1, 0), (1, 1), (2, 1), (2, 0), (3, 0), (3, 1), (0, 1))


def place(block, r):
    z, chip, core = block // 16, (block // 2) % 8, block % 2
    y, z_lo = PATH[chip]
    return device(z, y, r, 2 * z_lo + (core ^ (chip % 2)))


FAR = (1, 3, 0, 2)


def quarter_of(q, v, j):
    return (q + FAR[v ^ j]) % 4


def spread(x, j):
    perm = [(device(z, y, q, v), place(16 * z + 4 * y + q, quarter_of(q, v, j))) for z, y, q, v in CELLS]
    return lax.ppermute(x, AXES, perm)


def collect(x, j):
    perm = [(place(16 * z + 4 * y + q, quarter_of(q, v, j)), device(z, y, q, v)) for z, y, q, v in CELLS]
    return lax.ppermute(x, AXES, perm)


def view_swap(x, mask):
    return lax.ppermute(x, AXES, [(device(z, y, c, v), device(z, y, c, v ^ mask)) for z, y, c, v in CELLS])


def to_layer(x, step):
    perm = [(place(b, r), place((b + step) % 64, r)) for b in range(64) for r in range(4)]
    return lax.ppermute(x, AXES, perm)


def swap_row(x, j):
    other = (1, 0, 3, 2) if j == 0 else (0, 2, 1, 3)
    perm = [(place(b, r), place(b, other[r])) for b in range(64) for r in range(4)]
    return lax.ppermute(x, AXES, perm)


def position():
    blk, view = lax.axis_index("blk"), lax.axis_index("view")
    y = lax.rem(lax.div(blk, 4), 4)
    near = jnp.where(y < 2, y, y + 2)
    far = jnp.where(y == 0, 7, jnp.where(y == 3, 6, y + 1))
    chip = jnp.where(view < 2, near, far)
    core = (view & 1) ^ (chip & 1)
    return view, lax.rem(blk, 4), lax.div(blk, 16) * 16 + 2 * chip + core


def quarter_at(j):
    q = lax.rem(lax.axis_index("blk"), 4)
    slot = lax.axis_index("view") ^ j
    far = jnp.where(slot == 0, 1, jnp.where(slot == 1, 3, jnp.where(slot == 2, 0, 2)))
    return lax.rem(q + far, 4)


def view_at(j):
    _, r, block = position()
    far = lax.rem(r - lax.rem(block, 4) + 4, 4)
    return jnp.where(far == 1, 0, jnp.where(far == 3, 1, jnp.where(far == 0, 2, 3))) ^ j


def by_parity(index, first, second):
    return jnp.where((index & 1) == 0, first, second)


def vmem():
    return pl.BlockSpec(memory_space=pltpu.VMEM)


def smem():
    return pl.BlockSpec(memory_space=pltpu.SMEM)


def hbm():
    return pl.BlockSpec(memory_space=pl.ANY)


def call(body, outs, args, specs, scratch, flops, out_specs=None, mib=48):
    size = sum(a.size * a.dtype.itemsize for a in args)
    return pl.pallas_call(
        body,
        out_shape=outs,
        in_specs=specs,
        out_specs=out_specs or jax.tree.map(lambda _: vmem(), outs),
        scratch_shapes=scratch,
        compiler_params=pltpu.CompilerParams(vmem_limit_bytes=mib * 1024 * 1024),
        cost_estimate=pl.CostEstimate(flops=flops, bytes_accessed=size, transcendentals=0),
    )(*args)


def shape(*dims, dtype=F32):
    return jax.ShapeDtypeStruct(dims, dtype)


def iota(dims, axis):
    return lax.broadcasted_iota(jnp.int32, dims, axis)


def pieces(x):
    high = x.astype(BF16)
    low = (x - high.astype(F32)).astype(BF16)
    return high, low


def start_body(est, ext, sem):
    def window(k):
        first = max(0, k * ROWS - EDGE)
        size = min(LANES, (k + 1) * ROWS + EDGE) - first
        skip = first - (k * ROWS - EDGE)
        return pltpu.make_async_copy(est.at[:, pl.ds(first, size)], ext.at[:, pl.ds(skip, size)], sem)

    for k in range(VIEWS):

        @pl.when(quarter_at(0) == k)
        def _(k=k):
            window(k).start()
            if k == 0:
                ext[:, :EDGE, :] = jnp.zeros((BZ, EDGE, LANES), F32)
            if k == VIEWS - 1:
                ext[:, EXT - EDGE :, :] = jnp.zeros((BZ, EDGE, LANES), F32)
            window(k).wait()


def planes_body(offsets, weight, rec, psf_z, psf_y, psf_x, o0, o1, o2, o3, moved):
    dy, dx = offsets[0, 1], offsets[0, 2]
    row = iota((LANES, LANES), 0) + dy
    col = iota((LANES, LANES), 1) + dx
    inside = (row >= 0) & (row < LANES) & (col >= 0) & (col < LANES)
    back_y = lax.rem(LANES - dy, LANES)
    back_x = lax.rem(LANES - dx, LANES)

    @pl.loop(0, BZ, unroll=4)
    def _(z):
        plane = pltpu.roll(pltpu.roll(rec[0, z], back_y, 0), back_x, 1)
        moved[z] = jnp.where(inside, plane, 0.0)

    hz, hy, hx = (t[...] / jnp.sum(t[...], axis=1, keepdims=True) for t in (psf_z, psf_y, psf_x))
    lane = iota((1, LANES), 1)
    misc = jnp.where(lane == 0, weight[0], jnp.where(lane == 1, offsets[0, 0].astype(F32), 0.0))
    for j, out in enumerate((o0, o1, o2, o3)):
        start = pl.multiple_of(quarter_at(j) * ROWS, ROWS)
        out[:FLAT] = moved[:, pl.ds(start, ROWS), :].reshape(FLAT, LANES)
        out[FLAT:] = jnp.zeros((8, LANES), F32)
        for row, value in ((HZ, hz), (HY, hy), (HX, hx), (WZ, weight[0] * hz)):
            out[FLAT + row : FLAT + row + 1, :TAPS] = value
        out[FLAT + MISC : FLAT + MISC + 1, :] = misc


def shift_of(taps, v):
    return taps[v, MISC, 1].astype(jnp.int32)


def pack_body(a0, a1, a2, a3, up, down, taps, held, sems, tap_sems):
    blocks = (a0, a1, a2, a3)
    data, rows = [], []
    for j, a in enumerate(blocks):
        data.append(pltpu.make_async_copy(a.at[pl.ds(0, FLAT)], held.at[view_at(j)], sems.at[j]))
        rows.append(pltpu.make_async_copy(a.at[pl.ds(FLAT, 8)], taps.at[view_at(j)], tap_sems.at[j]))
    for copy in rows + data:
        copy.start()
    for copy in rows + data:
        copy.wait()
    for out in (up, down):
        out[FLAT:] = jnp.zeros((2 * FLAT, LANES), F32)
    n_up, n_down = jnp.int32(0), jnp.int32(0)
    for v in range(VIEWS):
        dz = shift_of(taps, v)

        @pl.when(dz < 0)
        def _(v=v, n=n_up):
            up[pl.ds(pl.multiple_of(n * FLAT, FLAT), FLAT)] = held[v]

        @pl.when(dz > 0)
        def _(v=v, n=n_down):
            down[pl.ds(pl.multiple_of(n * FLAT, FLAT), FLAT)] = held[v]

        n_up = n_up + jnp.where(dz < 0, 1, 0)
        n_down = n_down + jnp.where(dz > 0, 1, 0)


def bands_body(taps, wy_f, wy_b, wx_f, wx_b):
    dims = (ROWS, 4 * EXT)
    lane = iota(dims, 1)
    gap = (lane & (EXT - 1)) - iota(dims, 0) - 1
    for v in range(VIEWS):
        band = jnp.zeros(dims, F32)
        for a in range(TAPS):
            band = jnp.where(gap == a, taps[v, HY, a], band)
        high = band.astype(BF16).astype(F32)
        wy_f[v * ROWS : (v + 1) * ROWS, :] = jnp.where(lane < 2 * EXT, high, band - high).astype(BF16)

    dims = (EXT, LANES)
    lane = iota(dims, 1)
    gap = iota(dims, 0) - (lane & (ROWS - 1)) - 1
    band = jnp.zeros(dims, F32)
    for a in range(TAPS):
        tap = jnp.zeros((1, LANES), F32)
        for v in range(VIEWS):
            tap = jnp.where(iota((1, LANES), 1) >= v * ROWS, taps[v, HY, a], tap)
        band = jnp.where(gap == a, tap, band)
    high, low = pieces(band)
    wy_b[...] = jnp.concatenate([jnp.concatenate([high, high], 1), jnp.concatenate([low, low], 1)], 0)

    dims = (LANES, LANES)
    gap = iota(dims, 0) - iota(dims, 1)
    for v in range(VIEWS):
        for out, sign in ((wx_f, 1), (wx_b, -1)):
            band = jnp.zeros(dims, F32)
            for a in range(TAPS):
                band = jnp.where(gap == sign * (a - HALF), taps[v, HX, a], band)
            high, low = pieces(band)
            part = jnp.concatenate([high, low], 1)
            out[v] = jnp.concatenate([part, part], 0)


def forward_body(taps, before, own, after, wy_f, wx_f, out, inner, summed):
    _, _, block = position()

    def layer(k):
        if k < HALF:
            return jnp.where(block > 0, before[k + 1], 0.0)
        if k < HALF + BZ:
            return own[k - HALF]
        return jnp.where(block < 63, after[k - HALF - BZ], 0.0)

    for p in range(LAYERS // 2):
        high, low = pieces(jnp.concatenate([layer(2 * p), layer(2 * p + 1)], 1))
        data = jnp.concatenate([high, low, high, low], 0)
        done = jnp.dot(wy_f[...], data, preferred_element_type=F32)
        for v in range(VIEWS):
            rows = done[v * ROWS : (v + 1) * ROWS]
            inner[v, 2 * p] = rows[:, :LANES]
            inner[v, 2 * p + 1] = rows[:, LANES:]

    def sum_z(v):
        hz = [taps[v, HZ, a] for a in range(TAPS)]
        for t in range(ROWS // 8):
            rows = slice(8 * t, 8 * t + 8)
            acc = [None] * BZ
            for k in range(LAYERS):
                x = inner[v, k, rows, :]
                for i in range(max(0, k - TAPS + 1), min(BZ - 1, k) + 1):
                    term = hz[k - i] * x
                    acc[i] = term if acc[i] is None else acc[i] + term
            for i in range(BZ):
                summed[v, i, rows, :] = acc[i]

    def mix_x(v):
        high, low = pieces(summed[v].reshape(BZ * ROWS, LANES))
        done = jnp.dot(jnp.concatenate([high, low], 1), wx_f[v], preferred_element_type=F32)
        out[v] = (done[:, :LANES] + done[:, LANES:]).reshape(BZ, ROWS, LANES)

    for v in range(VIEWS):
        sum_z(v)
        if v > 0:
            mix_x(v - 1)
    mix_x(VIEWS - 1)


def back_body(taps, fwd, rec, wx_b, wy_b, before, own, after, inner, spread_z):
    def mix_x(v):
        ratio = (rec[v] / fwd[v]).reshape(BZ * ROWS, LANES)
        high, low = pieces(ratio)
        done = jnp.dot(jnp.concatenate([high, low], 1), wx_b[v], preferred_element_type=F32)
        inner[v] = (done[:, :LANES] + done[:, LANES:]).reshape(BZ, ROWS, LANES)

    def spread_layers(v):
        hz = [taps[v, WZ, a] for a in range(TAPS)]
        for t in range(ROWS // 8):
            x = [inner[v, i, 8 * t : 8 * t + 8, :] for i in range(BZ)]
            for k in range(LAYERS):
                acc = None
                for i in range(max(0, k - TAPS + 1), min(BZ - 1, k) + 1):
                    term = hz[k - i] * x[i]
                    acc = term if acc is None else acc + term
                spread_z[k, v * ROWS + 8 * t : v * ROWS + 8 * t + 8, :] = acc

    mix_x(0)
    for v in range(VIEWS):
        if v < VIEWS - 1:
            mix_x(v + 1)
        spread_layers(v)

    def store(k, value):
        if k < HALF:
            before[k] = value
        elif k < HALF + BZ:
            own[k - HALF] = value
        else:
            after[k - HALF - BZ] = value

    for p in range(LAYERS // 2):
        high, low = pieces(jnp.concatenate([spread_z[2 * p], spread_z[2 * p + 1]], 1))
        done = jnp.dot(wy_b[...], jnp.concatenate([high, low], 0), preferred_element_type=F32)
        both = done[:EXT] + done[EXT:]
        store(2 * p, both[:, :LANES])
        store(2 * p + 1, both[:, LANES:])


def first_back_body(taps, fwd, a0, a1, a2, a3, lower, upper, wx_b, wy_b, *rest):
    before, own, after, rec, held, low, high, sems, inner, spread_z = rest
    _, _, block = position()
    copies = [pltpu.make_async_copy(lower, low, sems.at[4]), pltpu.make_async_copy(upper, high, sems.at[5])]
    for j, a in enumerate((a0, a1, a2, a3)):
        copies.append(pltpu.make_async_copy(a.at[pl.ds(0, FLAT)], held.at[view_at(j)], sems.at[j]))
    for copy in copies:
        copy.start()
    for copy in copies:
        copy.wait()
    n_up, n_down = jnp.int32(0), jnp.int32(0)
    for v in range(VIEWS):
        dz = shift_of(taps, v)

        @pl.loop(0, BZ, unroll=8)
        def _(i, v=v, dz=dz, n_up=n_up, n_down=n_down):
            src = i + dz
            place_z = block * BZ + src

            def rows(layer, count):
                return pl.ds(pl.multiple_of(jnp.clip(layer, 0, count - 1) * ROWS, ROWS), ROWS)

            x = held[v, rows(src, BZ), :]
            x = jnp.where(src < 0, low[rows(n_up * BZ + src + BZ, 3 * BZ), :], x)
            x = jnp.where(src >= BZ, high[rows(n_down * BZ + src - BZ, 3 * BZ), :], x)
            rec[v, i] = jnp.where((place_z >= 0) & (place_z < 64 * BZ), x, 0.0)

        n_up = n_up + jnp.where(dz < 0, 1, 0)
        n_down = n_down + jnp.where(dz > 0, 1, 0)

    back_body(taps, fwd, rec, wx_b, wy_b, before, own, after, inner, spread_z)


def add_layers(own, from_prev, from_next, cut):
    _, _, block = position()
    out = []
    for i in range(BZ):
        value = own[i, cut]
        if i < HALF:
            value = value + jnp.where(block > 0, from_prev[i, cut], 0.0)
        if i > 0:
            value = value + jnp.where(block < 63, from_next[i - 1, cut], 0.0)
        out.append(value)
    return out


def halves_body(own, from_prev, from_next, s0, s1):
    _, r, _ = position()
    low, high = (add_layers(own, from_prev, from_next, cut) for cut in (slice(0, ROWS), slice(ROWS, EXT)))
    for i in range(BZ):
        s0[i] = by_parity(r, high[i], low[i])
        s1[i] = by_parity(r, low[i], high[i])


def edges_body(own, from_prev, from_next, s0, middle, s1):
    _, r, _ = position()
    cuts = (slice(0, EDGE), slice(EDGE, EXT - EDGE), slice(EXT - EDGE, EXT))
    low, center, high = (add_layers(own, from_prev, from_next, cut) for cut in cuts)
    for i in range(BZ):
        s0[i] = by_parity(r, high[i], low[i])
        s1[i] = by_parity(r, low[i], high[i])
        middle[i] = center[i]


def view_sum(taps):
    return taps[0, MISC, 0] + taps[1, MISC, 0] + taps[2, MISC, 0] + taps[3, MISC, 0]


def window_body(taps, ext, s0, s1, r0, r1, out):
    _, r, _ = position()
    wsum = view_sum(taps)
    for i in range(BZ):
        total = by_parity(r, s1[i], s0[i]) + jnp.where(r > 0, by_parity(r, r1[i], r0[i]), 0.0)
        out[i, :ROWS] = ext[i, :ROWS] * total / wsum
        total = by_parity(r, s0[i], s1[i]) + jnp.where(r < 3, by_parity(r, r0[i], r1[i]), 0.0)
        out[i, ROWS:] = ext[i, ROWS:] * total / wsum


def last_body(taps, ext, middle, r0, r1, out):
    _, r, _ = position()
    wsum = view_sum(taps)
    for i in range(BZ):
        total = middle[i, :EDGE] + jnp.where(r > 0, by_parity(r, r1[i], r0[i]), 0.0)
        out[i, :EDGE] = ext[i, EDGE:ROWS] * total / wsum
        total = middle[i, EDGE:] + jnp.where(r < 3, by_parity(r, r0[i], r1[i]), 0.0)
        out[i, EDGE:] = ext[i, ROWS : EXT - EDGE] * total / wsum


def join_body(c0, c1, c2, c3, out):
    for mask, chunk in enumerate((c0, c1, c2, c3)):
        start = pl.multiple_of(quarter_at(mask) * ROWS, ROWS)
        out[:, pl.ds(start, ROWS), :] = chunk[...]


BLOCK = (VIEWS, BZ, ROWS, LANES)
INNER = (VIEWS, LAYERS, ROWS, LANES)
SPREAD = (LAYERS, LANES, LANES)
WINDOW = (BZ, EXT, LANES)
HALO = (HALF, EXT, LANES)
QUARTER = (BZ, ROWS, LANES)
PACKED = (3 * FLAT, LANES)
STRIP = (BZ, EDGE, LANES)


def per_device(estimate, recorded, offsets, psf_z, psf_y, psf_x, view_weights):
    with jax.named_scope("window"):
        ext = call(start_body, shape(*WINDOW), (estimate,), [hbm()], [pltpu.SemaphoreType.DMA], 1_000_000)
        ext = spread(ext, 0)
    with jax.named_scope("planes"):
        chunks = call(
            planes_body,
            (shape(FLAT + 8, LANES),) * 4,
            (offsets, view_weights, recorded, psf_z, psf_y, psf_x),
            [smem(), smem()] + [vmem()] * 4,
            [pltpu.VMEM((BZ, LANES, LANES), F32)],
            10_000_000,
        )
    with jax.named_scope("spread"):
        mine = [spread(c, j) for j, c in enumerate(chunks)]
    with jax.named_scope("layers_in"):
        before = to_layer(ext, 1)
        after = to_layer(ext, -1)
    with jax.named_scope("shift"):
        up, down, taps = call(
            pack_body,
            (shape(*PACKED), shape(*PACKED), shape(VIEWS, 8, LANES)),
            tuple(mine),
            [hbm()] * 4,
            [pltpu.VMEM((VIEWS, FLAT, LANES), F32), pltpu.SemaphoreType.DMA((4,)), pltpu.SemaphoreType.DMA((4,))],
            8_000_000_000,
            (vmem(), vmem(), smem()),
        )
        lower = to_layer(up, 1)
        upper = to_layer(down, -1)

    with jax.named_scope("bands"):
        wy_f, wy_b, wx_f, wx_b = call(
            bands_body,
            (
                shape(LANES, 4 * EXT, dtype=BF16),
                shape(LANES, 2 * LANES, dtype=BF16),
                shape(VIEWS, 2 * LANES, 2 * LANES, dtype=BF16),
                shape(VIEWS, 2 * LANES, 2 * LANES, dtype=BF16),
            ),
            (taps,),
            [smem()],
            [],
            30_000_000,
        )

    rec = None
    for step in range(ITERS):
        if step > 0:
            with jax.named_scope("layers_in"):
                before = to_layer(ext, 1)
                after = to_layer(ext, -1)
        with jax.named_scope("forward"):
            fwd = call(
                forward_body,
                shape(*BLOCK),
                (taps, before, ext, after, wy_f, wx_f),
                [smem()] + [vmem()] * 5,
                [pltpu.VMEM(INNER, F32), pltpu.VMEM(BLOCK, F32)],
                20_000_000_000 if step == 0 else 2_000_000_000,
            )
        with jax.named_scope("back"):
            outs = (shape(*HALO), shape(*WINDOW), shape(*HALO))
            scratch = [pltpu.VMEM(BLOCK, F32), pltpu.VMEM(SPREAD, F32)]
            if rec is None:
                c_before, c_own, c_after, rec = call(
                    first_back_body,
                    outs + (shape(*BLOCK),),
                    (taps, fwd, *mine, lower, upper, wx_b, wy_b),
                    [smem(), vmem()] + [hbm()] * 6 + [vmem()] * 2,
                    [
                        pltpu.VMEM((VIEWS, FLAT, LANES), F32),
                        pltpu.VMEM(PACKED, F32),
                        pltpu.VMEM(PACKED, F32),
                        pltpu.SemaphoreType.DMA((6,)),
                    ]
                    + scratch,
                    2_000_000_000,
                )
            else:
                c_before, c_own, c_after = call(
                    back_body,
                    outs,
                    (taps, fwd, rec, wx_b, wy_b),
                    [smem()] + [vmem()] * 4,
                    scratch,
                    2_000_000_000,
                )
        with jax.named_scope("layers_out"):
            from_next = to_layer(c_before, -1)
            from_prev = to_layer(c_after, 1)
        if step < ITERS - 1:
            with jax.named_scope("rows"):
                low, high = call(
                    halves_body, (shape(*QUARTER),) * 2, (c_own, from_prev, from_next), [vmem()] * 3, [], 1_000_000
                )
                row_prev = swap_row(low, 0)
                row_next = swap_row(high, 1)
                ext = call(
                    window_body,
                    shape(*WINDOW),
                    (taps, ext, low, high, row_prev, row_next),
                    [smem()] + [vmem()] * 5,
                    [],
                    1_000_000,
                )
        else:
            with jax.named_scope("rows"):
                low, middle, high = call(
                    edges_body,
                    (shape(*STRIP), shape(*QUARTER), shape(*STRIP)),
                    (c_own, from_prev, from_next),
                    [vmem()] * 3,
                    [],
                    1_000_000,
                )
                row_prev = swap_row(low, 0)
                row_next = swap_row(high, 1)
                own = call(
                    last_body,
                    shape(*QUARTER),
                    (taps, ext, middle, row_prev, row_next),
                    [smem()] + [vmem()] * 4,
                    [],
                    1_000_000,
                )

    with jax.named_scope("result"):
        c0 = collect(own, 0)
        c1 = view_swap(c0, 1)
        c2 = collect(own, 2)
        c3 = view_swap(c2, 1)
        return call(join_body, shape(BZ, LANES, LANES), (c0, c1, c2, c3), [vmem()] * 4, [], 1_000_000)


def solution(mesh):
    in_specs = (
        P("blk", None, None),
        P("view", "blk", None, None),
        P("view", None),
        P("view", None),
        P("view", None),
        P("view", None),
        P("view"),
    )
    out_specs = P("blk", None, None)
    return jax.shard_map(
        per_device, mesh=mesh, in_specs=in_specs, out_specs=out_specs, check_vma=False
    )
```
